32 devices in a mesh: tm: 8 (over z, x), rows: 4 (over y, core).
Axes of the slice: x: 2, y: 2, z: 4, core: 2. Of those that a mesh axis runs over, the one named last changes fastest.
Arguments:
- features: bfloat16 [16, 4, 160, 512], P('tm', 'rows'), may hold values from -25 to 25
- norm_gain: float32 [512], replicated, may hold values from 0.1 to 1.9
- norm_bias: float32 [512], replicated, may hold values from -1 to 1
- weight: bfloat16 [3, 3, 3, 512, 256], replicated, may hold values from -0.0546875 to 0.0546875
- upstream: bfloat16 [16, 4, 160, 256], P('tm', 'rows'), may hold values from -20 to 20
Outputs:
- grad_features: bfloat16 [16, 4, 160, 512], P('tm', 'rows')
- grad_weight: float32 [3, 3, 3, 512, 256], P(None, None, None, 'tm', 'rows')
- grad_gain: float32 [512], replicated
- grad_bias: float32 [512], replicated
The draws below stay inside these ranges and needn't reach their ends.
All inputs are finite; a program needn't handle non-finite values.
Results may differ from the reference program's by a relative error of at most 0.0015.
Values may be sent and summed in bfloat16 or wider, within the bound.
A program may use at most 64 MiB of HBM per device.

```python
import jax
import jax.numpy as jnp
from jax import lax

C = 512
CO = 256
GROUPS = 32
CLIPS = 1
TF = 2
HD = 1
W = 160
FRAMES = 16
CLIP_FRAMES = 16
H = 4


def draw_features(key, part):
    keys = jax.random.split(key, 4)
    shape_all = (FRAMES, H, W, C)
    position = (jnp.arange(FRAMES) % CLIP_FRAMES).astype(jnp.float32) / max(CLIP_FRAMES - 1, 1)
    ramp = (1.0 + 2.0 * position)[:, None, None, None]
    chan_scale = jnp.exp(jax.random.uniform(keys[2], (C,), jnp.float32, -0.7, 0.7))
    blocks = H // HD
    order = jax.random.permutation(keys[3], blocks).astype(jnp.float32)
    level = order / max(blocks - 1, 1)
    block_of_row = jnp.arange(H) // HD
    row_level = jnp.take(level, block_of_row)
    row_scale = jnp.power(0.35, row_level)[None, :, None, None]
    base = jnp.clip(jax.random.normal(keys[0], shape_all, jnp.float32), -4.0, 4.0)
    return (base * ramp * chan_scale * row_scale).astype(jnp.bfloat16)


def draw_upstream(key, part):
    keys = jax.random.split(key, 3)
    shape_all = (FRAMES, H, W, CO)
    chan_offset = 0.4 * jnp.clip(jax.random.normal(keys[1], (CO,), jnp.float32), -3.0, 3.0)
    base = jnp.clip(jax.random.normal(keys[0], shape_all, jnp.float32), -5.0, 5.0)
    chosen = jax.random.permutation(keys[2], CO)
    frame_block = jnp.arange(FRAMES) // TF
    target = jnp.take(chosen, frame_block % CO)
    marked = (jnp.arange(CO)[None, :] == target[:, None]).astype(jnp.float32)
    boost = (1.0 + 2.0 * marked)[:, None, None, :]
    return ((base + chan_offset) * boost).astype(jnp.bfloat16)


def noise(rng, extent, width, reach, dtype=jnp.bfloat16):
    result = jax.random.normal(rng, extent, jnp.float32) * width
    return jnp.minimum(jnp.maximum(result, -reach), reach).astype(dtype)


def setup_inputs(seed: int = 0) -> dict:
    arg_keys = jax.random.split(jax.random.key(seed), 6)
    return {
        "features": draw_features(jax.random.fold_in(arg_keys[5], 71), 0),
        "norm_gain": jnp.clip(1.0 + 0.18 * jax.random.normal(arg_keys[1], (C,), jnp.float32), 0.1, 1.9),
        "norm_bias": jnp.clip(jax.random.uniform(arg_keys[2], (C,), jnp.float32, -1.0, 1.0), -1.0, 1.0),
        "weight": noise(arg_keys[3], (3, 3, 3, C, CO), (27 * C) ** -0.5, 0.0546875),
        "upstream": draw_upstream(jax.random.fold_in(arg_keys[5], 71), 0),
    }


epsilon = 1e-06

def reference(features, norm_gain, norm_bias, weight, upstream):
    group_size = C // GROUPS
    floats = features.astype(jnp.float32)
    grouped = floats.reshape(CLIPS, CLIP_FRAMES, H, W, GROUPS, group_size)
    centre_val = lax.optimization_barrier(jnp.mean(grouped, axis=(1, 2, 3, 5), keepdims=True))
    diffs = grouped - centre_val
    spread = lax.optimization_barrier(jnp.mean(diffs * diffs, axis=(1, 2, 3, 5), keepdims=True))
    inverse = lax.rsqrt(spread + epsilon)
    normed = (diffs * inverse).reshape(CLIPS, CLIP_FRAMES, H, W, C)
    preact = normed * norm_gain + norm_bias
    sig_val = jax.nn.sigmoid(preact)
    hidden = (preact * sig_val).astype(jnp.bfloat16)
    padded = jnp.concatenate([hidden[:, :1], hidden[:, :1], hidden], axis=1)
    padded = jnp.pad(padded, ((0, 0), (0, 0), (1, 1), (1, 1), (0, 0)))
    up_clips = upstream.reshape(CLIPS, CLIP_FRAMES, H, W, CO)
    up_flat = up_clips.reshape(-1, CO)
    grad_taps = []
    for time_tap in range(3):
        for row_tap in range(3):
            for col_tap in range(3):
                slab = padded[:, time_tap:time_tap + CLIP_FRAMES, row_tap:row_tap + H, col_tap:col_tap + W].reshape(-1, C)
                grad_taps.append(lax.dot_general(slab, up_flat, (((0,), (0,)), ((), ())), preferred_element_type=jnp.float32))
    grad_weight = jnp.stack(grad_taps).reshape(3, 3, 3, C, CO)
    up_padded = jnp.pad(up_clips, ((0, 0), (2, 2), (1, 1), (1, 1), (0, 0)))
    dense = jnp.zeros((CLIPS * (CLIP_FRAMES + 2) * H * W, C), jnp.float32)
    for time_tap in range(3):
        for row_tap in range(3):
            for col_tap in range(3):
                slab = up_padded[:, 2 - time_tap:4 - time_tap + CLIP_FRAMES, 2 - row_tap:2 - row_tap + H, 2 - col_tap:2 - col_tap + W].reshape(-1, CO)
                dense = dense + jnp.dot(slab, weight[time_tap, row_tap, col_tap].T, preferred_element_type=jnp.float32)
    dense = dense.reshape(CLIPS, CLIP_FRAMES + 2, H, W, C)
    grad_hidden = dense[:, 2:].at[:, 0].add(dense[:, 0] + dense[:, 1])
    grad_act = grad_hidden * sig_val * (1.0 + preact * (1.0 - sig_val))
    clip_gain = lax.optimization_barrier(jnp.sum(grad_act * normed, axis=(1, 2, 3)))
    clip_bias = lax.optimization_barrier(jnp.sum(grad_act, axis=(1, 2, 3)))
    grad_gain = lax.optimization_barrier(jnp.sum(clip_gain, axis=0))
    grad_bias = lax.optimization_barrier(jnp.sum(clip_bias, axis=0))
    count_clip = CLIP_FRAMES * H * W * group_size
    first_term = jnp.repeat(lax.optimization_barrier(jnp.sum((norm_gain * clip_bias).reshape(CLIPS, GROUPS, group_size), axis=2)) / count_clip, group_size, axis=1)
    second_term = jnp.repeat(lax.optimization_barrier(jnp.sum((norm_gain * clip_gain).reshape(CLIPS, GROUPS, group_size), axis=2)) / count_clip, group_size, axis=1)
    inverse_chan = jnp.repeat(inverse.reshape(CLIPS, GROUPS), group_size, axis=1)
    first_term = first_term[:, None, None, None, :]
    second_term = second_term[:, None, None, None, :]
    inverse_chan = inverse_chan[:, None, None, None, :]
    grad_features = (inverse_chan * (grad_act * norm_gain - first_term - normed * second_term)).astype(jnp.bfloat16)
    return (grad_features.reshape(FRAMES, H, W, C), grad_weight, grad_gain, grad_bias)
```

```python
import functools

import jax
import jax.numpy as jnp
from jax import lax
from jax.experimental import pallas as pl
from jax.experimental.pallas import tpu as pltpu
from jax.sharding import PartitionSpec as P

GROUPS = 32
CLIPS = 1


epsilon = 1e-06


def from_behind(value, axis, steps):
    count = lax.axis_size(axis)
    initial, last = (max(0, -steps), min(count, count - steps))
    return lax.ppermute(value, axis, [(source, source + steps) for source in range(initial, last)])


def padded(cells, sides, width):
    for axis, dim in sides:
        count = lax.axis_size(axis)
        ends = count - 1
        head = lax.slice_in_dim(cells, 0, width, axis=dim)
        tail = lax.slice_in_dim(cells, cells.shape[dim] - width, cells.shape[dim], axis=dim)
        cells = jnp.concatenate(
            [
                lax.ppermute(tail, axis, [(i, (i + 1) % count) for i in range(ends)]),
                cells,
                lax.ppermute(head, axis, [((i + 1) % count, i) for i in range(ends)]),
            ],
            axis=dim,
        )
    return cells


def on_device(features, norm_gain, norm_bias, weight, upstream):
    frames_dev, rows_dev, cols, chans = features.shape
    outs = upstream.shape[3]
    group_size = chans // GROUPS
    per_clip = lax.axis_size("tm") // CLIPS
    time_index = lax.axis_index("tm")
    clip_index = time_index // per_clip
    first_dev = time_index % per_clip == 0
    last_dev = time_index % per_clip == per_clip - 1
    selector = (jnp.arange(CLIPS) == clip_index).astype(jnp.float32)
    count_clip = frames_dev * rows_dev * cols * group_size * per_clip * lax.axis_size("rows")
    floats = features.astype(jnp.float32)
    grouped = floats.reshape(frames_dev, rows_dev, cols, GROUPS, group_size)
    local_sum = jnp.sum(grouped, axis=(0, 1, 2, 4))
    local_sq = jnp.sum(grouped * grouped, axis=(0, 1, 2, 4))
    total_sum, total_sq = lax.psum(
        (selector[:, None] * local_sum, selector[:, None] * local_sq), ("tm", "rows")
    )
    centre_val = jnp.sum(selector[:, None] * total_sum, axis=0) / count_clip
    spread = jnp.sum(selector[:, None] * total_sq, axis=0) / count_clip - centre_val * centre_val
    diffs = grouped - centre_val[:, None]
    inverse = lax.rsqrt(spread + epsilon)
    normed = (diffs * inverse[:, None]).reshape(frames_dev, rows_dev, cols, chans)
    preact = normed * norm_gain + norm_bias
    sig_val = jax.nn.sigmoid(preact)
    hidden = (preact * sig_val).astype(jnp.bfloat16)
    earlier = from_behind(hidden, "tm", 1)
    earlier = jnp.where(first_dev, jnp.concatenate([hidden[:1], hidden[:1]], axis=0), earlier)
    extended = jnp.concatenate([earlier, hidden], axis=0)
    extended = padded(extended, (("rows", 1),), 1)
    extended = jnp.pad(extended, ((0, 0), (0, 0), (1, 1), (0, 0)))
    up_flat = upstream.reshape(-1, outs)
    grad_taps = []
    for time_tap in range(3):
        for row_tap in range(3):
            for col_tap in range(3):
                slab = extended[
                    time_tap : time_tap + frames_dev,
                    row_tap : row_tap + rows_dev,
                    col_tap : col_tap + cols,
                ].reshape(-1, chans)
                grad_taps.append(
                    lax.dot_general(
                        slab, up_flat, (((0,), (0,)), ((), ())), preferred_element_type=jnp.float32
                    )
                )
    local_grad = jnp.stack(grad_taps).reshape(3, 3, 3, chans, outs)
    halfway = lax.psum_scatter(local_grad, "tm", scatter_dimension=3, tiled=True)
    grad_weight = lax.psum_scatter(halfway, "rows", scatter_dimension=4, tiled=True)
    later = from_behind(upstream, "tm", -1)
    later = jnp.where(last_dev, jnp.zeros_like(later), later)
    up_ext = jnp.concatenate([upstream, later], axis=0)
    up_ext = padded(up_ext, (("rows", 1),), 1)
    up_ext = jnp.pad(up_ext, ((0, 0), (0, 0), (1, 1), (0, 0)))
    dense = jnp.zeros((frames_dev * rows_dev * cols, chans), jnp.float32)
    for time_tap in range(3):
        for row_tap in range(3):
            for col_tap in range(3):
                slab = up_ext[
                    2 - time_tap : 2 - time_tap + frames_dev,
                    2 - row_tap : 2 - row_tap + rows_dev,
                    2 - col_tap : 2 - col_tap + cols,
                ].reshape(-1, outs)
                dense = dense + jnp.dot(
                    slab, weight[time_tap, row_tap, col_tap].T, preferred_element_type=jnp.float32
                )
    dense = dense.reshape(frames_dev, rows_dev, cols, chans)

    def pad_terms(unused):
        total = jnp.zeros((rows_dev * cols, chans), jnp.float32)
        for row_tap in range(3):
            for col_tap in range(3):
                first_slab = up_ext[
                    0, 2 - row_tap : 2 - row_tap + rows_dev, 2 - col_tap : 2 - col_tap + cols
                ].reshape(-1, outs)
                second_slab = up_ext[
                    1, 2 - row_tap : 2 - row_tap + rows_dev, 2 - col_tap : 2 - col_tap + cols
                ].reshape(-1, outs)
                total = total + jnp.dot(
                    first_slab, weight[0, row_tap, col_tap].T, preferred_element_type=jnp.float32
                )
                total = total + jnp.dot(
                    first_slab, weight[1, row_tap, col_tap].T, preferred_element_type=jnp.float32
                )
                total = total + jnp.dot(
                    second_slab, weight[0, row_tap, col_tap].T, preferred_element_type=jnp.float32
                )
        return total.reshape(rows_dev, cols, chans)

    def skip_terms(unused):
        return jnp.zeros((rows_dev, cols, chans), jnp.float32)

    extra = lax.cond(first_dev, pad_terms, skip_terms, 0)
    grad_hidden = dense.at[0].add(extra)
    grad_act = grad_hidden * sig_val * (1.0 + preact * (1.0 - sig_val))
    local_gain = jnp.sum(grad_act * normed, axis=(0, 1, 2))
    local_bias = jnp.sum(grad_act, axis=(0, 1, 2))
    clip_gain, clip_bias = lax.psum(
        (selector[:, None] * local_gain, selector[:, None] * local_bias), ("tm", "rows")
    )
    grad_gain = jnp.sum(clip_gain, axis=0)
    grad_bias = jnp.sum(clip_bias, axis=0)
    own_gain = jnp.sum(selector[:, None] * clip_gain, axis=0)
    own_bias = jnp.sum(selector[:, None] * clip_bias, axis=0)
    first_term = jnp.repeat(
        jnp.sum((norm_gain * own_bias).reshape(GROUPS, -1), axis=1) / count_clip, group_size
    )
    second_term = jnp.repeat(
        jnp.sum((norm_gain * own_gain).reshape(GROUPS, -1), axis=1) / count_clip, group_size
    )
    inverse_chan = jnp.repeat(inverse, group_size)
    grad_features = (
        inverse_chan * (grad_act * norm_gain - first_term - normed * second_term)
    ).astype(jnp.bfloat16)
    return (grad_features, grad_weight, grad_gain, grad_bias)


MESH = pl.DeviceIdType.MESH
F32 = jnp.float32
BF16 = jnp.bfloat16


def group_total(value, group_size):
    lanes = value.shape[1]
    lane = lax.broadcasted_iota(jnp.int32, value.shape, 1)
    step = 1
    while step < group_size:
        up = pltpu.roll(value, step, 1)
        down = pltpu.roll(value, lanes - step, 1)
        value = value + jnp.where((lane & step) != 0, up, down)
        step *= 2
    return value


def pack_pair(first, second):
    lane = lax.broadcasted_iota(jnp.int32, first.shape, 1)
    low = lane < 64
    even = jnp.where(low, first, pltpu.roll(second, 64, 1))
    odd = jnp.where(low, pltpu.roll(first, 64, 1), second)
    return even.astype(BF16), odd.astype(BF16)


def kernel(
    dims,
    feat, gain_ref, bias_ref, weight_hbm, up_ref,
    gf_ref, gw_ref, gg_ref, gb_ref,
    weight, ext, acc, normed_s, dact_s, hpack, hall, upack, uall, ut, gacc,
    st_r, st_t, sg_r, sg_t,
    w_sem,
    st_rs, st_rr, st_ts, st_tr, sg_rs, sg_rr, sg_ts, sg_tr,
    ha_s, ha_r, u1_s, u1_r, u2_s, u2_r, h1_s, h1_r, h2_s, h2_r,
):
    nt, nr, cols, chans, outs, group_size = dims
    pos = 2 * cols
    a = lax.axis_index("tm")
    b = lax.axis_index("rows")
    count = float(nt * nr * pos * group_size)

    w_copy = pltpu.make_async_copy(weight_hbm, weight, w_sem)
    w_copy.start()

    barrier = pltpu.get_barrier_semaphore()
    tm_peers = [lax.rem(a + d, nt) for d in range(1, nt)]
    row_peers = [lax.rem(b + d, nr) for d in range(1, nr)]
    for peer in row_peers:
        pl.semaphore_signal(barrier, inc=1, device_id=(a, peer), device_id_type=MESH)
    for peer in tm_peers:
        pl.semaphore_signal(barrier, inc=1, device_id=(peer, b), device_id_type=MESH)

    def to_row(src, dst, ssem, rsem, peer):
        return pltpu.make_async_remote_copy(
            src_ref=src, dst_ref=dst, send_sem=ssem, recv_sem=rsem,
            device_id=(a, peer), device_id_type=MESH,
        )

    def to_tm(src, dst, ssem, rsem, peer):
        return pltpu.make_async_remote_copy(
            src_ref=src, dst_ref=dst, send_sem=ssem, recv_sem=rsem,
            device_id=(peer, b), device_id_type=MESH,
        )

    xs = feat[...].astype(F32)
    st_r[b, 0:1] = jnp.sum(xs, axis=0, keepdims=True)
    st_r[b, 1:2] = jnp.sum(xs * xs, axis=0, keepdims=True)
    st_r[b, 2:8] = jnp.zeros((6, chans), F32)

    for q in range(outs // 128):
        lanes = slice(q * 128, q * 128 + 128)
        even, odd = pack_pair(
            up_ref[0:cols, lanes].astype(F32), up_ref[cols:pos, lanes].astype(F32)
        )
        upack[2 * q] = even
        upack[2 * q + 1] = odd
    ext[1, 0:pos] = up_ref[...]
    zeros_ext = jnp.zeros((pos, outs), BF16)

    @pl.when(b == 0)
    def _():
        ext[0, 0:pos] = zeros_ext

    @pl.when(b == nr - 1)
    def _():
        ext[2, 0:pos] = zeros_ext

    @pl.when(a == nt - 1)
    def _():
        for r in range(3):
            ext[r, pos : 2 * pos] = zeros_ext

    pl.semaphore_wait(barrier, nt + nr - 2)

    for peer in row_peers:
        to_row(st_r.at[b], st_r.at[b], st_rs.at[peer], st_rr.at[b], peer).start()

    def u1_copy(src_row, peer):
        return to_row(
            upack.at[peer], uall.at[src_row, pl.ds(a * cols, cols)],
            u1_s.at[peer], u1_r.at[src_row], peer,
        )

    for peer in row_peers:
        u1_copy(b, peer).start()
    own = pl.ds(pl.multiple_of(a * cols, 32), cols)
    uall[b, own] = upack[b]

    def to_above():
        return to_row(up_ref, ext.at[2, pl.ds(0, pos)], ha_s.at[0], ha_r.at[0], lax.rem(b + nr - 1, nr))

    def to_below():
        return to_row(up_ref, ext.at[0, pl.ds(0, pos)], ha_s.at[1], ha_r.at[1], lax.rem(b + 1, nr))

    @pl.when(b > 0)
    def _():
        to_above().start()

    @pl.when(b < nr - 1)
    def _():
        to_below().start()

    for peer in row_peers:
        to_row(st_r.at[b], st_r.at[peer], st_rs.at[peer], st_rr.at[peer], peer).wait_recv()
    part = st_r[0]
    for r in range(1, nr):
        part = part + st_r[r]
    st_t[a] = part
    for peer in tm_peers:
        to_tm(st_t.at[a], st_t.at[a], st_ts.at[peer], st_tr.at[a], peer).start()

    for peer in row_peers:
        u1_copy(peer, peer).wait_recv()

    def u2_copy(src, peer):
        place = pl.ds(src * cols, cols)
        return to_tm(
            uall.at[:, place], uall.at[:, place], u2_s.at[peer], u2_r.at[src], peer
        )

    for peer in tm_peers:
        to_tm(st_t.at[a], st_t.at[peer], st_ts.at[peer], st_tr.at[peer], peer).wait_recv()
    for peer in tm_peers:
        u2_copy(a, peer).start()
    total = st_t[0]
    for t in range(1, nt):
        total = total + st_t[t]
    total = group_total(total, group_size) / count
    centre = total[0:1]
    inverse = lax.rsqrt(total[1:2] - centre * centre + epsilon)
    gain = gain_ref[...]
    bias = bias_ref[...]
    for q in range(chans // 128):
        lanes = slice(q * 128, q * 128 + 128)
        halves = []
        for f in range(2):
            rows = slice(f * cols, f * cols + cols)
            normed = (feat[rows, lanes].astype(F32) - centre[:, lanes]) * inverse[:, lanes]
            preact = normed * gain[:, lanes] + bias[:, lanes]
            sig = jax.nn.sigmoid(preact)
            normed_s[rows, lanes] = normed
            dact_s[rows, lanes] = sig * (1.0 + preact * (1.0 - sig))
            halves.append(preact * sig)
        even, odd = pack_pair(*halves)
        hpack[2 * q] = even
        hpack[2 * q + 1] = odd

    def h1_copy(src, peer):
        return to_tm(
            hpack.at[peer], hall.at[b, pl.ds((src + 1) * cols, cols)],
            h1_s.at[peer], h1_r.at[src], peer,
        )

    for peer in tm_peers:
        h1_copy(a, peer).start()
    hall[b, pl.ds(pl.multiple_of((a + 1) * cols, 32), cols)] = hpack[a]

    @pl.when(b > 0)
    def _():
        to_below().wait_recv()

    @pl.when(b < nr - 1)
    def _():
        to_above().wait_recv()

    def to_earlier():
        return to_tm(
            ext.at[:, pl.ds(0, pos)], ext.at[:, pl.ds(pos, pos)], ha_s.at[2], ha_r.at[2], lax.rem(a + nt - 1, nt)
        )

    @pl.when(a > 0)
    def _():
        to_earlier().start()

    w_copy.wait()

    def dot_t(lhs, rhs):
        return lax.dot_general(lhs, rhs, (((1,), (1,)), ((), ())), preferred_element_type=F32)

    def dense_own(c, carry):
        val = dot_t(ext[2, 0:pos], weight[2, 0, c])
        for tap in range(1, 3):
            val = val + dot_t(ext[2 - tap, 0:pos], weight[2, tap, c])
        acc[c] = val
        return carry

    lax.fori_loop(0, 3, dense_own, 0)

    for peer in tm_peers:
        h1_copy(peer, peer).wait_recv()

    def h2_copy(src, peer):
        place = pl.ds(cols, nt * cols)
        return to_row(
            hall.at[src, place], hall.at[src, place], h2_s.at[peer], h2_r.at[src], peer
        )

    for peer in row_peers:
        h2_copy(b, peer).start()

    @pl.when(a < nt - 1)
    def _():
        to_earlier().wait_recv()

    def dense_rest(c, carry):
        val = acc[c]
        for tap in range(3):
            val = val + dot_t(ext[2 - tap, cols : cols + pos], weight[1, tap, c])
            val = val + dot_t(ext[2 - tap, pos : 2 * pos], weight[0, tap, c])
        acc[c] = val
        return carry

    lax.fori_loop(0, 3, dense_rest, 0)

    @pl.when(a == 0)
    def _():
        def dense_first(c, carry):
            val = acc[c, 0:cols]
            for tap in range(3):
                val = val + dot_t(ext[2 - tap, 0:cols], weight[0, tap, c])
                val = val + dot_t(ext[2 - tap, 0:cols], weight[1, tap, c])
                val = val + dot_t(ext[2 - tap, cols:pos], weight[0, tap, c])
            acc[c, 0:cols] = val
            return carry

        lax.fori_loop(0, 3, dense_first, 0)

    sg_r[b, 2:8] = jnp.zeros((6, chans), F32)
    for q in range(chans // 128):
        lanes = slice(q * 128, q * 128 + 128)
        sum_gain = jnp.zeros((1, 128), F32)
        sum_bias = jnp.zeros((1, 128), F32)
        for f in range(2):
            rows = slice(f * cols, f * cols + cols)
            place = lax.broadcasted_iota(jnp.int32, (cols, 128), 0)
            right = jnp.where(
                place == cols - 1, 0.0, pltpu.roll(acc[0, rows, lanes], cols - 1, 0)
            )
            left = jnp.where(place == 0, 0.0, pltpu.roll(acc[2, rows, lanes], 1, 0))
            act = (acc[1, rows, lanes] + right + left) * dact_s[rows, lanes]
            dact_s[rows, lanes] = act
            sum_gain = sum_gain + jnp.sum(act * normed_s[rows, lanes], axis=0, keepdims=True)
            sum_bias = sum_bias + jnp.sum(act, axis=0, keepdims=True)
        sg_r[b, 0:1, lanes] = sum_gain
        sg_r[b, 1:2, lanes] = sum_bias
    for peer in row_peers:
        to_row(sg_r.at[b], sg_r.at[b], sg_rs.at[peer], sg_rr.at[b], peer).start()

    for peer in tm_peers:
        u2_copy(peer, peer).wait_recv()
    half = nt * cols // 2
    for part_index in range(2):
        rows = slice(part_index * half, part_index * half + half)
        place = lax.broadcasted_iota(jnp.int32, (half, 128), 0) % cols

        def turn(i, carry, rows=rows, place=place):
            block = uall[i, rows].astype(F32)
            ahead = jnp.where(place == cols - 1, 0.0, pltpu.roll(block, half - 1, 0))
            behind = jnp.where(place == 0, 0.0, pltpu.roll(block, 1, 0))
            ut[i, 0:128, rows] = ahead.T.astype(BF16)
            ut[i, 128:256, rows] = block.T.astype(BF16)
            ut[i, 256:384, rows] = behind.T.astype(BF16)
            return carry

        lax.fori_loop(0, nr, turn, 0)

    for peer in row_peers:
        to_row(sg_r.at[b], sg_r.at[peer], sg_rs.at[peer], sg_rr.at[peer], peer).wait_recv()
    part = sg_r[0]
    for r in range(1, nr):
        part = part + sg_r[r]
    sg_t[a] = part
    for peer in tm_peers:
        to_tm(sg_t.at[a], sg_t.at[a], sg_ts.at[peer], sg_tr.at[a], peer).start()

    for peer in row_peers:
        h2_copy(peer, peer).wait_recv()
    low = lax.broadcasted_iota(jnp.int32, (cols, 128), 1) < 64
    for r in range(nr):
        block = hall[r, cols : 2 * cols].astype(F32)
        hall[r, 0:cols] = jnp.where(low, block, pltpu.roll(block, 64, 1)).astype(BF16)
    span = nt * cols
    for r in range(nr):
        both = jnp.concatenate([hall[r, 0:span], hall[r, cols : cols + span]], axis=1)
        for tap in range(3):
            i = r - tap + 1
            if 0 <= i < nr:
                prod = jnp.dot(ut[i], both, preferred_element_type=F32)
                first = r == max(0, tap - 1)
                gacc[tap] = prod if first else gacc[tap] + prod
    for tap in range(3):
        for c in range(3):
            base = c * 128
            even = gacc[tap, base : base + 64]
            odd = gacc[tap, base + 64 : base + 128]
            turned = (even + pltpu.roll(odd, 192, 1)).T
            for t in range(3):
                gw_ref[t * 9 + tap * 3 + c] = turned[t * 64 : t * 64 + 64]

    for peer in tm_peers:
        to_tm(sg_t.at[a], sg_t.at[peer], sg_ts.at[peer], sg_tr.at[peer], peer).wait_recv()
    total = sg_t[0]
    for t in range(1, nt):
        total = total + sg_t[t]
    gg_ref[...] = total[0:1]
    gb_ref[...] = total[1:2]
    terms = group_total(total * gain, group_size) / count
    second_term = terms[0:1]
    first_term = terms[1:2]
    for q in range(chans // 128):
        lanes = slice(q * 128, q * 128 + 128)
        gf_ref[:, lanes] = (
            inverse[:, lanes]
            * (
                dact_s[:, lanes] * gain[:, lanes]
                - first_term[:, lanes]
                - normed_s[:, lanes] * second_term[:, lanes]
            )
        ).astype(BF16)

    for peer in row_peers:
        to_row(st_r.at[b], st_r.at[b], st_rs.at[peer], st_rr.at[b], peer).wait_send()
        to_row(sg_r.at[b], sg_r.at[b], sg_rs.at[peer], sg_rr.at[b], peer).wait_send()
        u1_copy(b, peer).wait_send()
        h2_copy(b, peer).wait_send()
    for peer in tm_peers:
        to_tm(st_t.at[a], st_t.at[a], st_ts.at[peer], st_tr.at[a], peer).wait_send()
        to_tm(sg_t.at[a], sg_t.at[a], sg_ts.at[peer], sg_tr.at[a], peer).wait_send()
        u2_copy(a, peer).wait_send()
        h1_copy(a, peer).wait_send()

    @pl.when(b > 0)
    def _():
        to_above().wait_send()

    @pl.when(b < nr - 1)
    def _():
        to_below().wait_send()

    @pl.when(a > 0)
    def _():
        to_earlier().wait_send()


def fused(features, norm_gain, norm_bias, weight, upstream):
    frames_dev, rows_dev, cols, chans = features.shape
    outs = upstream.shape[3]
    nt, nr = lax.axis_size("tm"), lax.axis_size("rows")
    pos = frames_dev * rows_dev * cols
    dims = (nt, nr, cols, chans, outs, chans // GROUPS)
    vmem = pl.BlockSpec(memory_space=pltpu.VMEM)
    dma = pltpu.SemaphoreType.DMA
    span = nt * cols
    gf, gw, gg, gb = pl.pallas_call(
        functools.partial(kernel, dims),
        out_shape=(
            jax.ShapeDtypeStruct((pos, chans), BF16),
            jax.ShapeDtypeStruct((27, 64, 64), F32),
            jax.ShapeDtypeStruct((1, chans), F32),
            jax.ShapeDtypeStruct((1, chans), F32),
        ),
        in_specs=[vmem, vmem, vmem, pl.BlockSpec(memory_space=pl.ANY), vmem],
        out_specs=(vmem, vmem, vmem, vmem),
        scratch_shapes=[
            pltpu.VMEM((3, 3, 3, chans, outs), BF16),
            pltpu.VMEM((3, 2 * pos, outs), BF16),
            pltpu.VMEM((3, pos, chans), F32),
            pltpu.VMEM((pos, chans), F32),
            pltpu.VMEM((pos, chans), F32),
            pltpu.VMEM((nt, cols, 128), BF16),
            pltpu.VMEM((nr, span + cols, 128), BF16),
            pltpu.VMEM((nr, cols, 128), BF16),
            pltpu.VMEM((nr, span, 128), BF16),
            pltpu.VMEM((nr, 384, span), BF16),
            pltpu.VMEM((3, 384, 256), F32),
            pltpu.VMEM((nr, 8, chans), F32),
            pltpu.VMEM((nt, 8, chans), F32),
            pltpu.VMEM((nr, 8, chans), F32),
            pltpu.VMEM((nt, 8, chans), F32),
            dma,
            dma((nr,)), dma((nr,)), dma((nt,)), dma((nt,)),
            dma((nr,)), dma((nr,)), dma((nt,)), dma((nt,)),
            dma((3,)), dma((3,)),
            dma((nr,)), dma((nr,)), dma((nt,)), dma((nt,)),
            dma((nt,)), dma((nt,)), dma((nr,)), dma((nr,)),
        ],
        compiler_params=pltpu.CompilerParams(
            collective_id=0, has_side_effects=True, vmem_limit_bytes=48 * 1024 * 1024
        ),
    )(
        features.reshape(pos, chans),
        norm_gain.reshape(1, chans),
        norm_bias.reshape(1, chans),
        weight,
        upstream.reshape(pos, outs),
    )
    return (
        gf.reshape(features.shape),
        gw.reshape(3, 3, 3, 64, 64),
        gg.reshape(chans),
        gb.reshape(chans),
    )


def body(features, norm_gain, norm_bias, weight, upstream):
    frames_dev, rows_dev, cols, chans = features.shape
    outs = upstream.shape[3]
    nt, nr = lax.axis_size("tm"), lax.axis_size("rows")
    fits = (
        CLIPS == 1
        and (frames_dev, rows_dev) == (2, 1)
        and (chans, outs) == (64 * nt, 64 * nr)
        and cols % 32 == 0
        and (nt * cols) % 256 == 0
    )
    run = fused if fits else on_device
    return run(features, norm_gain, norm_bias, weight, upstream)


def solution(mesh):
    in_specs = (P("tm", "rows", None, None), P(), P(), P(), P("tm", "rows", None, None))
    out_specs = (P("tm", "rows", None, None), P(None, None, None, "tm", "rows"), P(), P())
    return jax.shard_map(
        body, mesh=mesh, in_specs=in_specs, out_specs=out_specs, check_vma=False
    )
```

```python
import functools

import jax
import jax.numpy as jnp
from jax import lax
from jax.experimental import pallas as pl
from jax.experimental.pallas import tpu as pltpu
from jax.sharding import PartitionSpec as P

GROUPS = 32
CLIPS = 1


epsilon = 1e-06


def from_behind(value, axis, steps):
    count = lax.axis_size(axis)
    initial, last = (max(0, -steps), min(count, count - steps))
    return lax.ppermute(value, axis, [(source, source + steps) for source in range(initial, last)])


def padded(cells, sides, width):
    for axis, dim in sides:
        count = lax.axis_size(axis)
        ends = count - 1
        head = lax.slice_in_dim(cells, 0, width, axis=dim)
        tail = lax.slice_in_dim(cells, cells.shape[dim] - width, cells.shape[dim], axis=dim)
        cells = jnp.concatenate(
            [
                lax.ppermute(tail, axis, [(i, (i + 1) % count) for i in range(ends)]),
                cells,
                lax.ppermute(head, axis, [((i + 1) % count, i) for i in range(ends)]),
            ],
            axis=dim,
        )
    return cells


def on_device(features, norm_gain, norm_bias, weight, upstream):
    frames_dev, rows_dev, cols, chans = features.shape
    outs = upstream.shape[3]
    group_size = chans // GROUPS
    per_clip = lax.axis_size("tm") // CLIPS
    time_index = lax.axis_index("tm")
    clip_index = time_index // per_clip
    first_dev = time_index % per_clip == 0
    last_dev = time_index % per_clip == per_clip - 1
    selector = (jnp.arange(CLIPS) == clip_index).astype(jnp.float32)
    count_clip = frames_dev * rows_dev * cols * group_size * per_clip * lax.axis_size("rows")
    floats = features.astype(jnp.float32)
    grouped = floats.reshape(frames_dev, rows_dev, cols, GROUPS, group_size)
    local_sum = jnp.sum(grouped, axis=(0, 1, 2, 4))
    local_sq = jnp.sum(grouped * grouped, axis=(0, 1, 2, 4))
    total_sum, total_sq = lax.psum(
        (selector[:, None] * local_sum, selector[:, None] * local_sq), ("tm", "rows")
    )
    centre_val = jnp.sum(selector[:, None] * total_sum, axis=0) / count_clip
    spread = jnp.sum(selector[:, None] * total_sq, axis=0) / count_clip - centre_val * centre_val
    diffs = grouped - centre_val[:, None]
    inverse = lax.rsqrt(spread + epsilon)
    normed = (diffs * inverse[:, None]).reshape(frames_dev, rows_dev, cols, chans)
    preact = normed * norm_gain + norm_bias
    sig_val = jax.nn.sigmoid(preact)
    hidden = (preact * sig_val).astype(jnp.bfloat16)
    earlier = from_behind(hidden, "tm", 1)
    earlier = jnp.where(first_dev, jnp.concatenate([hidden[:1], hidden[:1]], axis=0), earlier)
    extended = jnp.concatenate([earlier, hidden], axis=0)
    extended = padded(extended, (("rows", 1),), 1)
    extended = jnp.pad(extended, ((0, 0), (0, 0), (1, 1), (0, 0)))
    up_flat = upstream.reshape(-1, outs)
    grad_taps = []
    for time_tap in range(3):
        for row_tap in range(3):
            for col_tap in range(3):
                slab = extended[
                    time_tap : time_tap + frames_dev,
                    row_tap : row_tap + rows_dev,
                    col_tap : col_tap + cols,
                ].reshape(-1, chans)
                grad_taps.append(
                    lax.dot_general(
                        slab, up_flat, (((0,), (0,)), ((), ())), preferred_element_type=jnp.float32
                    )
                )
    local_grad = jnp.stack(grad_taps).reshape(3, 3, 3, chans, outs)
    halfway = lax.psum_scatter(local_grad, "tm", scatter_dimension=3, tiled=True)
    grad_weight = lax.psum_scatter(halfway, "rows", scatter_dimension=4, tiled=True)
    later = from_behind(upstream, "tm", -1)
    later = jnp.where(last_dev, jnp.zeros_like(later), later)
    up_ext = jnp.concatenate([upstream, later], axis=0)
    up_ext = padded(up_ext, (("rows", 1),), 1)
    up_ext = jnp.pad(up_ext, ((0, 0), (0, 0), (1, 1), (0, 0)))
    dense = jnp.zeros((frames_dev * rows_dev * cols, chans), jnp.float32)
    for time_tap in range(3):
        for row_tap in range(3):
            for col_tap in range(3):
                slab = up_ext[
                    2 - time_tap : 2 - time_tap + frames_dev,
                    2 - row_tap : 2 - row_tap + rows_dev,
                    2 - col_tap : 2 - col_tap + cols,
                ].reshape(-1, outs)
                dense = dense + jnp.dot(
                    slab, weight[time_tap, row_tap, col_tap].T, preferred_element_type=jnp.float32
                )
    dense = dense.reshape(frames_dev, rows_dev, cols, chans)

    def pad_terms(unused):
        total = jnp.zeros((rows_dev * cols, chans), jnp.float32)
        for row_tap in range(3):
            for col_tap in range(3):
                first_slab = up_ext[
                    0, 2 - row_tap : 2 - row_tap + rows_dev, 2 - col_tap : 2 - col_tap + cols
                ].reshape(-1, outs)
                second_slab = up_ext[
                    1, 2 - row_tap : 2 - row_tap + rows_dev, 2 - col_tap : 2 - col_tap + cols
                ].reshape(-1, outs)
                total = total + jnp.dot(
                    first_slab, weight[0, row_tap, col_tap].T, preferred_element_type=jnp.float32
                )
                total = total + jnp.dot(
                    first_slab, weight[1, row_tap, col_tap].T, preferred_element_type=jnp.float32
                )
                total = total + jnp.dot(
                    second_slab, weight[0, row_tap, col_tap].T, preferred_element_type=jnp.float32
                )
        return total.reshape(rows_dev, cols, chans)

    def skip_terms(unused):
        return jnp.zeros((rows_dev, cols, chans), jnp.float32)

    extra = lax.cond(first_dev, pad_terms, skip_terms, 0)
    grad_hidden = dense.at[0].add(extra)
    grad_act = grad_hidden * sig_val * (1.0 + preact * (1.0 - sig_val))
    local_gain = jnp.sum(grad_act * normed, axis=(0, 1, 2))
    local_bias = jnp.sum(grad_act, axis=(0, 1, 2))
    clip_gain, clip_bias = lax.psum(
        (selector[:, None] * local_gain, selector[:, None] * local_bias), ("tm", "rows")
    )
    grad_gain = jnp.sum(clip_gain, axis=0)
    grad_bias = jnp.sum(clip_bias, axis=0)
    own_gain = jnp.sum(selector[:, None] * clip_gain, axis=0)
    own_bias = jnp.sum(selector[:, None] * clip_bias, axis=0)
    first_term = jnp.repeat(
        jnp.sum((norm_gain * own_bias).reshape(GROUPS, -1), axis=1) / count_clip, group_size
    )
    second_term = jnp.repeat(
        jnp.sum((norm_gain * own_gain).reshape(GROUPS, -1), axis=1) / count_clip, group_size
    )
    inverse_chan = jnp.repeat(inverse, group_size)
    grad_features = (
        inverse_chan * (grad_act * norm_gain - first_term - normed * second_term)
    ).astype(jnp.bfloat16)
    return (grad_features, grad_weight, grad_gain, grad_bias)


MESH = pl.DeviceIdType.MESH
F32 = jnp.float32
BF16 = jnp.bfloat16


def group_total(value, group_size):
    lanes = value.shape[1]
    lane = lax.broadcasted_iota(jnp.int32, value.shape, 1)
    step = 1
    while step < group_size:
        up = pltpu.roll(value, step, 1)
        down = pltpu.roll(value, lanes - step, 1)
        value = value + jnp.where((lane & step) != 0, up, down)
        step *= 2
    return value


def pack_pair(first, second):
    lane = lax.broadcasted_iota(jnp.int32, first.shape, 1)
    low = lane < 64
    even = jnp.where(low, first, pltpu.roll(second, 64, 1))
    odd = jnp.where(low, pltpu.roll(first, 64, 1), second)
    return even.astype(BF16), odd.astype(BF16)


def kernel(
    dims,
    feat_hbm, gain_hbm, bias_hbm, weight_hbm, up_hbm,
    gf_ref, gw_ref, gg_ref, gb_ref,
    feat, gain_ref, bias_ref, up_ref, weight, ext, acc, normed_s, dact_s, hpack, hall, upack, uall, ut, gacc,
    st_r, st_t, sg_r, sg_t,
    in_sem,
    st_rs, st_rr, st_ts, st_tr, sg_rs, sg_rr, sg_ts, sg_tr,
    ha_s, ha_r, u1_s, u1_r, u2_s, u2_r, u3_s, h1_s, h1_r, hc_s, hc_r, hy_s, hy_r, hf_s, hf_r,
):
    nt, nr, cols, chans, outs, group_size = dims
    pos = 2 * cols
    a = lax.axis_index("tm")
    b = lax.axis_index("rows")
    count = float(nt * nr * pos * group_size)

    nq = chans // 128
    f_copy = pltpu.make_async_copy(feat_hbm, feat, in_sem.at[0])
    c_copy = pltpu.make_async_copy(up_hbm, up_ref, in_sem.at[1])
    g_copy = pltpu.make_async_copy(gain_hbm, gain_ref, in_sem.at[2])
    b_copy = pltpu.make_async_copy(bias_hbm, bias_ref, in_sem.at[3])
    w_copy = pltpu.make_async_copy(weight_hbm, weight, in_sem.at[4])
    f_copy.start()
    c_copy.start()
    g_copy.start()
    b_copy.start()

    barrier = pltpu.get_barrier_semaphore()
    tm_peers = [lax.rem(a + d, nt) for d in range(1, nt)]
    row_peers = [lax.rem(b + d, nr) for d in range(1, nr)]
    line_peers = [lax.rem(a + d, nt) for d in range(2, nt, 2)]
    side = a + 1 - 2 * lax.rem(a, 2)
    twin = b + 1 - 2 * lax.rem(b, 2)
    across = lax.rem(b + 2, nr)
    far = lax.rem(twin + 2, nr)
    for peer in row_peers:
        pl.semaphore_signal(barrier, inc=1, device_id=(a, peer), device_id_type=MESH)
    for peer in tm_peers:
        pl.semaphore_signal(barrier, inc=1, device_id=(peer, b), device_id_type=MESH)

    def to_row(src, dst, ssem, rsem, peer):
        return pltpu.make_async_remote_copy(
            src_ref=src, dst_ref=dst, send_sem=ssem, recv_sem=rsem,
            device_id=(a, peer), device_id_type=MESH,
        )

    def to_tm(src, dst, ssem, rsem, peer):
        return pltpu.make_async_remote_copy(
            src_ref=src, dst_ref=dst, send_sem=ssem, recv_sem=rsem,
            device_id=(peer, b), device_id_type=MESH,
        )

    f_copy.wait()
    w_copy.start()
    for q in range(nq):
        xs = feat[:, q * 128 : q * 128 + 128].astype(F32)
        st_r[b, q : q + 1] = jnp.sum(xs, axis=0, keepdims=True)
        st_r[b, nq + q : nq + q + 1] = jnp.sum(xs * xs, axis=0, keepdims=True)
    pl.semaphore_wait(barrier, nt + nr - 2)
    for peer in row_peers:
        to_row(st_r.at[b], st_r.at[b], st_rs.at[peer], st_rr.at[b], peer).start()

    c_copy.wait()
    for q in range(outs // 128):
        lanes = slice(q * 128, q * 128 + 128)
        even, odd = pack_pair(
            up_ref[0:cols, lanes].astype(F32), up_ref[cols:pos, lanes].astype(F32)
        )
        upack[2 * q] = even
        upack[2 * q + 1] = odd
    def u1_copy(src_row, peer):
        return to_row(
            upack.at[peer], uall.at[src_row, pl.ds(a * cols, cols)],
            u1_s.at[peer], u1_r.at[src_row], peer,
        )

    for peer in row_peers:
        u1_copy(b, peer).start()
    own = pl.ds(pl.multiple_of(a * cols, 32), cols)
    uall[b, own] = upack[b]

    here, ahead_rows = pl.ds(0, pos), pl.ds(pos, pos)
    above, below = lax.rem(b + nr - 1, nr), lax.rem(b + 1, nr)

    def to_above():
        return to_row(up_ref, ext.at[2, here], ha_s.at[0], ha_r.at[0], above)

    def to_below():
        return to_row(up_ref, ext.at[0, here], ha_s.at[1], ha_r.at[1], below)

    def to_earlier():
        return to_tm(
            up_ref, ext.at[1, ahead_rows], ha_s.at[2], ha_r.at[2], lax.rem(a + nt - 1, nt)
        )

    def next_above():
        return to_row(
            ext.at[1, ahead_rows], ext.at[2, ahead_rows], ha_s.at[3], ha_r.at[3], above
        )

    def next_below():
        return to_row(
            ext.at[1, ahead_rows], ext.at[0, ahead_rows], ha_s.at[4], ha_r.at[4], below
        )

    not_top, not_bottom = b > 0, b < nr - 1
    not_first, not_last = a > 0, a < nt - 1

    @pl.when(not_first)
    def _():
        to_earlier().start()

    @pl.when(not_top)
    def _():
        to_above().start()

    @pl.when(not_bottom)
    def _():
        to_below().start()

    ext[1, 0:pos] = up_ref[...]
    zeros_ext = jnp.zeros((2 * pos, outs), BF16)

    @pl.when(b == 0)
    def _():
        ext[0] = zeros_ext

    @pl.when(b == nr - 1)
    def _():
        ext[2] = zeros_ext

    @pl.when(a == nt - 1)
    def _():
        for r in range(3):
            ext[r, pos : 2 * pos] = zeros_ext[0:pos]

    for peer in row_peers:
        to_row(st_r.at[b], st_r.at[peer], st_rs.at[peer], st_rr.at[peer], peer).wait_recv()
    part = st_r[0]
    for r in range(1, nr):
        part = part + st_r[r]
    st_t[a] = part
    for peer in tm_peers:
        to_tm(st_t.at[a], st_t.at[a], st_ts.at[peer], st_tr.at[a], peer).start()

    for peer in row_peers:
        u1_copy(peer, peer).wait_recv()

    def u2_copy(src, peer):
        place = pl.ds(src * cols, cols)
        return to_tm(
            uall.at[:, place], uall.at[:, place], u2_s.at[peer], u2_r.at[src], peer
        )

    def u3_copy(src):
        place = pl.ds(src * cols, cols)
        return to_tm(
            uall.at[:, place], uall.at[:, place], u3_s.at[src], u2_r.at[src], side
        )

    for peer in line_peers:
        u2_copy(a, peer).start()
    u3_copy(a).start()

    for peer in tm_peers:
        to_tm(st_t.at[a], st_t.at[peer], st_ts.at[peer], st_tr.at[peer], peer).wait_recv()
    total = st_t[0]
    for t in range(1, nt):
        total = total + st_t[t]
    total = group_total(total, group_size) / count
    centre = total[0:nq]
    inverse = lax.rsqrt(total[nq : 2 * nq] - centre * centre + epsilon)
    g_copy.wait()
    b_copy.wait()
    for q in range(nq):
        lanes = slice(q * 128, q * 128 + 128)
        halves = []
        for f in range(2):
            rows = slice(f * cols, f * cols + cols)
            normed = (feat[rows, lanes].astype(F32) - centre[q : q + 1]) * inverse[q : q + 1]
            preact = normed * gain_ref[:, lanes] + bias_ref[:, lanes]
            sig = jax.nn.sigmoid(preact)
            normed_s[rows, lanes] = normed
            dact_s[rows, lanes] = sig * (1.0 + preact * (1.0 - sig))
            halves.append(preact * sig)
        even, odd = pack_pair(*halves)
        hpack[2 * q] = even
        hpack[2 * q + 1] = odd

    def h1_copy(src, peer):
        return to_tm(
            hpack.at[peer], hall.at[b, pl.ds((src + 1) * cols, cols)],
            h1_s.at[peer], h1_r.at[src], peer,
        )

    for peer in tm_peers:
        h1_copy(a, peer).start()
    hall[b, pl.ds(pl.multiple_of((a + 1) * cols, 32), cols)] = hpack[a]

    @pl.when(not_last)
    def _():
        to_earlier().wait_recv()

    @pl.when(not_last & not_top)
    def _():
        next_above().start()

    @pl.when(not_last & not_bottom)
    def _():
        next_below().start()

    @pl.when(not_top)
    def _():
        to_below().wait_recv()

    @pl.when(not_bottom)
    def _():
        to_above().wait_recv()

    w_copy.wait()

    def dot_t(lhs, rhs):
        return lax.dot_general(lhs, rhs, (((1,), (1,)), ((), ())), preferred_element_type=F32)

    def dense_own(c, carry):
        val = dot_t(ext[2, 0:pos], weight[2, 0, c])
        for tap in range(1, 3):
            val = val + dot_t(ext[2 - tap, 0:pos], weight[2, tap, c])
        acc[c] = val
        return carry

    lax.fori_loop(0, 3, dense_own, 0)

    for peer in line_peers:
        u2_copy(peer, peer).wait_recv()
        u3_copy(peer).start()

    def pass_on(row, src, ssem, rsem, peer):
        place = hall.at[row, pl.ds((src + 1) * cols, cols)]
        return to_row(place, place, ssem.at[src], rsem.at[src], peer)

    pass_on(b, a, hy_s, hy_r, across).start()
    pass_on(b, a, hc_s, hc_r, twin).start()
    for peer in tm_peers:
        h1_copy(peer, peer).wait_recv()
        pass_on(b, peer, hy_s, hy_r, across).start()
        pass_on(b, peer, hc_s, hc_r, twin).start()

    @pl.when(not_last & not_top)
    def _():
        next_below().wait_recv()

    @pl.when(not_last & not_bottom)
    def _():
        next_above().wait_recv()

    def dense_rest(c, carry):
        val = acc[c]
        for tap in range(3):
            val = val + dot_t(ext[2 - tap, cols : cols + pos], weight[1, tap, c])
            val = val + dot_t(ext[2 - tap, pos : 2 * pos], weight[0, tap, c])
        acc[c] = val
        return carry

    lax.fori_loop(0, 3, dense_rest, 0)

    @pl.when(a == 0)
    def _():
        def dense_first(c, carry):
            val = acc[c, 0:cols]
            for tap in range(3):
                val = val + dot_t(ext[2 - tap, 0:cols], weight[0, tap, c])
                val = val + dot_t(ext[2 - tap, 0:cols], weight[1, tap, c])
                val = val + dot_t(ext[2 - tap, cols:pos], weight[0, tap, c])
            acc[c, 0:cols] = val
            return carry

        lax.fori_loop(0, 3, dense_first, 0)

    for src in [a] + tm_peers:
        pass_on(across, src, hy_s, hy_r, across).wait_recv()
        pass_on(across, src, hf_s, hf_r, twin).start()

    for q in range(chans // 128):
        lanes = slice(q * 128, q * 128 + 128)
        sum_gain = jnp.zeros((1, 128), F32)
        sum_bias = jnp.zeros((1, 128), F32)
        for f in range(2):
            rows = slice(f * cols, f * cols + cols)
            place = lax.broadcasted_iota(jnp.int32, (cols, 128), 0)
            right = jnp.where(
                place == cols - 1, 0.0, pltpu.roll(acc[0, rows, lanes], cols - 1, 0)
            )
            left = jnp.where(place == 0, 0.0, pltpu.roll(acc[2, rows, lanes], 1, 0))
            act = (acc[1, rows, lanes] + right + left) * dact_s[rows, lanes]
            dact_s[rows, lanes] = act
            sum_gain = sum_gain + jnp.sum(act * normed_s[rows, lanes], axis=0, keepdims=True)
            sum_bias = sum_bias + jnp.sum(act, axis=0, keepdims=True)
        sg_r[b, q : q + 1] = sum_gain
        sg_r[b, nq + q : nq + q + 1] = sum_bias
    for peer in row_peers:
        to_row(sg_r.at[b], sg_r.at[b], sg_rs.at[peer], sg_rr.at[b], peer).start()

    for src in [side] + [lax.rem(side + d, nt) for d in range(2, nt, 2)]:
        u3_copy(src).wait_recv()
    half = nt * cols // 2
    for part_index in range(2):
        rows = slice(part_index * half, part_index * half + half)
        place = lax.broadcasted_iota(jnp.int32, (half, 128), 0) % cols

        def turn(i, carry, rows=rows, place=place):
            block = uall[i, rows].astype(F32)
            ahead = jnp.where(place == cols - 1, 0.0, pltpu.roll(block, half - 1, 0))
            behind = jnp.where(place == 0, 0.0, pltpu.roll(block, 1, 0))
            ut[i, 0:128, rows] = ahead.T.astype(BF16)
            ut[i, 128:256, rows] = block.T.astype(BF16)
            ut[i, 256:384, rows] = behind.T.astype(BF16)
            return carry

        lax.fori_loop(0, nr, turn, 0)

    for peer in row_peers:
        to_row(sg_r.at[b], sg_r.at[peer], sg_rs.at[peer], sg_rr.at[peer], peer).wait_recv()
    part = sg_r[0]
    for r in range(1, nr):
        part = part + sg_r[r]
    sg_t[a] = part
    for peer in tm_peers:
        to_tm(sg_t.at[a], sg_t.at[a], sg_ts.at[peer], sg_tr.at[a], peer).start()

    for src in [a] + tm_peers:
        pass_on(twin, src, hc_s, hc_r, twin).wait_recv()
        pass_on(far, src, hf_s, hf_r, twin).wait_recv()
    low = lax.broadcasted_iota(jnp.int32, (cols, 128), 1) < 64
    for r in range(nr):
        block = hall[r, cols : 2 * cols].astype(F32)
        hall[r, 0:cols] = jnp.where(low, block, pltpu.roll(block, 64, 1)).astype(BF16)
    span = nt * cols
    for r in range(nr):
        both = jnp.concatenate([hall[r, 0:span], hall[r, cols : cols + span]], axis=1)
        for tap in range(3):
            i = r - tap + 1
            if 0 <= i < nr:
                prod = jnp.dot(ut[i], both, preferred_element_type=F32)
                first = r == max(0, tap - 1)
                gacc[tap] = prod if first else gacc[tap] + prod
    for tap in range(3):
        for c in range(3):
            base = c * 128
            even = gacc[tap, base : base + 64]
            odd = gacc[tap, base + 64 : base + 128]
            turned = (even + pltpu.roll(odd, 192, 1)).T
            for t in range(3):
                gw_ref[t * 9 + tap * 3 + c] = turned[t * 64 : t * 64 + 64]

    for peer in tm_peers:
        to_tm(sg_t.at[a], sg_t.at[peer], sg_ts.at[peer], sg_tr.at[peer], peer).wait_recv()
    total = sg_t[0]
    for t in range(1, nt):
        total = total + sg_t[t]
    for q in range(nq):
        lanes = slice(q * 128, q * 128 + 128)
        gain = gain_ref[:, lanes]
        gg_ref[:, lanes] = total[q : q + 1]
        gb_ref[:, lanes] = total[nq + q : nq + q + 1]
        second_term = group_total(total[q : q + 1] * gain, group_size) / count
        first_term = group_total(total[nq + q : nq + q + 1] * gain, group_size) / count
        gf_ref[:, lanes] = (
            inverse[q : q + 1]
            * (dact_s[:, lanes] * gain - first_term - normed_s[:, lanes] * second_term)
        ).astype(BF16)

    for peer in row_peers:
        to_row(st_r.at[b], st_r.at[b], st_rs.at[peer], st_rr.at[b], peer).wait_send()
        to_row(sg_r.at[b], sg_r.at[b], sg_rs.at[peer], sg_rr.at[b], peer).wait_send()
        u1_copy(b, peer).wait_send()
    for peer in tm_peers:
        to_tm(st_t.at[a], st_t.at[a], st_ts.at[peer], st_tr.at[a], peer).wait_send()
        to_tm(sg_t.at[a], sg_t.at[a], sg_ts.at[peer], sg_tr.at[a], peer).wait_send()
        h1_copy(a, peer).wait_send()
    u3_copy(a).wait_send()
    for peer in line_peers:
        u2_copy(a, peer).wait_send()
        u3_copy(peer).wait_send()
    for src in [a] + tm_peers:
        pass_on(b, src, hy_s, hy_r, across).wait_send()
        pass_on(b, src, hc_s, hc_r, twin).wait_send()
        pass_on(across, src, hf_s, hf_r, twin).wait_send()

    @pl.when(not_top)
    def _():
        to_above().wait_send()

    @pl.when(not_bottom)
    def _():
        to_below().wait_send()

    @pl.when(not_first)
    def _():
        to_earlier().wait_send()

    @pl.when(not_last & not_top)
    def _():
        next_above().wait_send()

    @pl.when(not_last & not_bottom)
    def _():
        next_below().wait_send()


def fused(features, norm_gain, norm_bias, weight, upstream):
    frames_dev, rows_dev, cols, chans = features.shape
    outs = upstream.shape[3]
    nt, nr = lax.axis_size("tm"), lax.axis_size("rows")
    pos = frames_dev * rows_dev * cols
    dims = (nt, nr, cols, chans, outs, chans // GROUPS)
    vmem = pl.BlockSpec(memory_space=pltpu.VMEM)
    dma = pltpu.SemaphoreType.DMA
    span = nt * cols
    gf, gw, gg, gb = pl.pallas_call(
        functools.partial(kernel, dims),
        out_shape=(
            jax.ShapeDtypeStruct((pos, chans), BF16),
            jax.ShapeDtypeStruct((27, 64, 64), F32),
            jax.ShapeDtypeStruct((1, chans), F32),
            jax.ShapeDtypeStruct((1, chans), F32),
        ),
        in_specs=[pl.BlockSpec(memory_space=pltpu.HBM)] * 5,
        out_specs=(vmem, vmem, vmem, vmem),
        scratch_shapes=[
            pltpu.VMEM((pos, chans), BF16),
            pltpu.VMEM((1, chans), F32),
            pltpu.VMEM((1, chans), F32),
            pltpu.VMEM((pos, outs), BF16),
            pltpu.VMEM((3, 3, 3, chans, outs), BF16),
            pltpu.VMEM((3, 2 * pos, outs), BF16),
            pltpu.VMEM((3, pos, chans), F32),
            pltpu.VMEM((pos, chans), F32),
            pltpu.VMEM((pos, chans), F32),
            pltpu.VMEM((nt, cols, 128), BF16),
            pltpu.VMEM((nr, span + cols, 128), BF16),
            pltpu.VMEM((nr, cols, 128), BF16),
            pltpu.VMEM((nr, span, 128), BF16),
            pltpu.VMEM((nr, 384, span), BF16),
            pltpu.VMEM((3, 384, 256), F32),
            pltpu.VMEM((nr, 8, 128), F32),
            pltpu.VMEM((nt, 8, 128), F32),
            pltpu.VMEM((nr, 8, 128), F32),
            pltpu.VMEM((nt, 8, 128), F32),
            dma((5,)),
            dma((nr,)), dma((nr,)), dma((nt,)), dma((nt,)),
            dma((nr,)), dma((nr,)), dma((nt,)), dma((nt,)),
            dma((5,)), dma((5,)),
            dma((nr,)), dma((nr,)), dma((nt,)), dma((nt,)), dma((nt,)),
            dma((nt,)), dma((nt,)), dma((nt,)), dma((nt,)),
            dma((nt,)), dma((nt,)), dma((nt,)), dma((nt,)),
        ],
        compiler_params=pltpu.CompilerParams(
            collective_id=0, has_side_effects=True, vmem_limit_bytes=48 * 1024 * 1024
        ),
    )(
        features.reshape(pos, chans),
        norm_gain.reshape(1, chans),
        norm_bias.reshape(1, chans),
        weight,
        upstream.reshape(pos, outs),
    )
    return (
        gf.reshape(features.shape),
        gw.reshape(3, 3, 3, 64, 64),
        gg.reshape(chans),
        gb.reshape(chans),
    )


def body(features, norm_gain, norm_bias, weight, upstream):
    frames_dev, rows_dev, cols, chans = features.shape
    outs = upstream.shape[3]
    nt, nr = lax.axis_size("tm"), lax.axis_size("rows")
    fits = (
        CLIPS == 1
        and (frames_dev, rows_dev) == (2, 1)
        and (nt, nr) == (8, 4)
        and (chans, outs) == (64 * nt, 64 * nr)
        and cols % 32 == 0
        and (nt * cols) % 256 == 0
    )
    run = fused if fits else on_device
    return run(features, norm_gain, norm_bias, weight, upstream)


def solution(mesh):
    in_specs = (P("tm", "rows", None, None), P(), P(), P(), P("tm", "rows", None, None))
    out_specs = (P("tm", "rows", None, None), P(None, None, None, "tm", "rows"), P(), P())
    return jax.shard_map(
        body, mesh=mesh, in_specs=in_specs, out_specs=out_specs, check_vma=False
    )
```

```python
import functools

import jax
import jax.numpy as jnp
from jax import lax
from jax.experimental import pallas as pl
from jax.experimental.pallas import tpu as pltpu
from jax.sharding import PartitionSpec as P

GROUPS = 32
CLIPS = 1


epsilon = 1e-06


def from_behind(value, axis, steps):
    count = lax.axis_size(axis)
    initial, last = (max(0, -steps), min(count, count - steps))
    return lax.ppermute(value, axis, [(source, source + steps) for source in range(initial, last)])


def padded(cells, sides, width):
    for axis, dim in sides:
        count = lax.axis_size(axis)
        ends = count - 1
        head = lax.slice_in_dim(cells, 0, width, axis=dim)
        tail = lax.slice_in_dim(cells, cells.shape[dim] - width, cells.shape[dim], axis=dim)
        cells = jnp.concatenate(
            [
                lax.ppermute(tail, axis, [(i, (i + 1) % count) for i in range(ends)]),
                cells,
                lax.ppermute(head, axis, [((i + 1) % count, i) for i in range(ends)]),
            ],
            axis=dim,
        )
    return cells


def on_device(features, norm_gain, norm_bias, weight, upstream):
    frames_dev, rows_dev, cols, chans = features.shape
    outs = upstream.shape[3]
    group_size = chans // GROUPS
    per_clip = lax.axis_size("tm") // CLIPS
    time_index = lax.axis_index("tm")
    clip_index = time_index // per_clip
    first_dev = time_index % per_clip == 0
    last_dev = time_index % per_clip == per_clip - 1
    selector = (jnp.arange(CLIPS) == clip_index).astype(jnp.float32)
    count_clip = frames_dev * rows_dev * cols * group_size * per_clip * lax.axis_size("rows")
    floats = features.astype(jnp.float32)
    grouped = floats.reshape(frames_dev, rows_dev, cols, GROUPS, group_size)
    local_sum = jnp.sum(grouped, axis=(0, 1, 2, 4))
    local_sq = jnp.sum(grouped * grouped, axis=(0, 1, 2, 4))
    total_sum, total_sq = lax.psum(
        (selector[:, None] * local_sum, selector[:, None] * local_sq), ("tm", "rows")
    )
    centre_val = jnp.sum(selector[:, None] * total_sum, axis=0) / count_clip
    spread = jnp.sum(selector[:, None] * total_sq, axis=0) / count_clip - centre_val * centre_val
    diffs = grouped - centre_val[:, None]
    inverse = lax.rsqrt(spread + epsilon)
    normed = (diffs * inverse[:, None]).reshape(frames_dev, rows_dev, cols, chans)
    preact = normed * norm_gain + norm_bias
    sig_val = jax.nn.sigmoid(preact)
    hidden = (preact * sig_val).astype(jnp.bfloat16)
    earlier = from_behind(hidden, "tm", 1)
    earlier = jnp.where(first_dev, jnp.concatenate([hidden[:1], hidden[:1]], axis=0), earlier)
    extended = jnp.concatenate([earlier, hidden], axis=0)
    extended = padded(extended, (("rows", 1),), 1)
    extended = jnp.pad(extended, ((0, 0), (0, 0), (1, 1), (0, 0)))
    up_flat = upstream.reshape(-1, outs)
    grad_taps = []
    for time_tap in range(3):
        for row_tap in range(3):
            for col_tap in range(3):
                slab = extended[
                    time_tap : time_tap + frames_dev,
                    row_tap : row_tap + rows_dev,
                    col_tap : col_tap + cols,
                ].reshape(-1, chans)
                grad_taps.append(
                    lax.dot_general(
                        slab, up_flat, (((0,), (0,)), ((), ())), preferred_element_type=jnp.float32
                    )
                )
    local_grad = jnp.stack(grad_taps).reshape(3, 3, 3, chans, outs)
    halfway = lax.psum_scatter(local_grad, "tm", scatter_dimension=3, tiled=True)
    grad_weight = lax.psum_scatter(halfway, "rows", scatter_dimension=4, tiled=True)
    later = from_behind(upstream, "tm", -1)
    later = jnp.where(last_dev, jnp.zeros_like(later), later)
    up_ext = jnp.concatenate([upstream, later], axis=0)
    up_ext = padded(up_ext, (("rows", 1),), 1)
    up_ext = jnp.pad(up_ext, ((0, 0), (0, 0), (1, 1), (0, 0)))
    dense = jnp.zeros((frames_dev * rows_dev * cols, chans), jnp.float32)
    for time_tap in range(3):
        for row_tap in range(3):
            for col_tap in range(3):
                slab = up_ext[
                    2 - time_tap : 2 - time_tap + frames_dev,
                    2 - row_tap : 2 - row_tap + rows_dev,
                    2 - col_tap : 2 - col_tap + cols,
                ].reshape(-1, outs)
                dense = dense + jnp.dot(
                    slab, weight[time_tap, row_tap, col_tap].T, preferred_element_type=jnp.float32
                )
    dense = dense.reshape(frames_dev, rows_dev, cols, chans)

    def pad_terms(unused):
        total = jnp.zeros((rows_dev * cols, chans), jnp.float32)
        for row_tap in range(3):
            for col_tap in range(3):
                first_slab = up_ext[
                    0, 2 - row_tap : 2 - row_tap + rows_dev, 2 - col_tap : 2 - col_tap + cols
                ].reshape(-1, outs)
                second_slab = up_ext[
                    1, 2 - row_tap : 2 - row_tap + rows_dev, 2 - col_tap : 2 - col_tap + cols
                ].reshape(-1, outs)
                total = total + jnp.dot(
                    first_slab, weight[0, row_tap, col_tap].T, preferred_element_type=jnp.float32
                )
                total = total + jnp.dot(
                    first_slab, weight[1, row_tap, col_tap].T, preferred_element_type=jnp.float32
                )
                total = total + jnp.dot(
                    second_slab, weight[0, row_tap, col_tap].T, preferred_element_type=jnp.float32
                )
        return total.reshape(rows_dev, cols, chans)

    def skip_terms(unused):
        return jnp.zeros((rows_dev, cols, chans), jnp.float32)

    extra = lax.cond(first_dev, pad_terms, skip_terms, 0)
    grad_hidden = dense.at[0].add(extra)
    grad_act = grad_hidden * sig_val * (1.0 + preact * (1.0 - sig_val))
    local_gain = jnp.sum(grad_act * normed, axis=(0, 1, 2))
    local_bias = jnp.sum(grad_act, axis=(0, 1, 2))
    clip_gain, clip_bias = lax.psum(
        (selector[:, None] * local_gain, selector[:, None] * local_bias), ("tm", "rows")
    )
    grad_gain = jnp.sum(clip_gain, axis=0)
    grad_bias = jnp.sum(clip_bias, axis=0)
    own_gain = jnp.sum(selector[:, None] * clip_gain, axis=0)
    own_bias = jnp.sum(selector[:, None] * clip_bias, axis=0)
    first_term = jnp.repeat(
        jnp.sum((norm_gain * own_bias).reshape(GROUPS, -1), axis=1) / count_clip, group_size
    )
    second_term = jnp.repeat(
        jnp.sum((norm_gain * own_gain).reshape(GROUPS, -1), axis=1) / count_clip, group_size
    )
    inverse_chan = jnp.repeat(inverse, group_size)
    grad_features = (
        inverse_chan * (grad_act * norm_gain - first_term - normed * second_term)
    ).astype(jnp.bfloat16)
    return (grad_features, grad_weight, grad_gain, grad_bias)


MESH = pl.DeviceIdType.MESH
F32 = jnp.float32
BF16 = jnp.bfloat16


def group_total(value, group_size):
    lanes = value.shape[1]
    lane = lax.broadcasted_iota(jnp.int32, value.shape, 1)
    step = 1
    while step < group_size:
        up = pltpu.roll(value, step, 1)
        down = pltpu.roll(value, lanes - step, 1)
        value = value + jnp.where((lane & step) != 0, up, down)
        step *= 2
    return value


def pack_pair(first, second):
    lane = lax.broadcasted_iota(jnp.int32, first.shape, 1)
    low = lane < 64
    even = jnp.where(low, first, pltpu.roll(second, 64, 1))
    odd = jnp.where(low, pltpu.roll(first, 64, 1), second)
    return even.astype(BF16), odd.astype(BF16)


def kernel(
    dims,
    feat_hbm, gain_hbm, bias_hbm, weight_hbm, up_hbm,
    gf_ref, gw_ref, gg_ref, gb_ref,
    feat, gain_ref, bias_ref, up_ref, weight, ext, acc, normed_s, dact_s, hpack, hall, upack, uall, ut, gacc,
    st_r, st_t, sg_r, sg_t,
    in_sem,
    st_rs, st_rr, st_ts, st_tr, sg_rs, sg_rr, sg_ts, sg_tr,
    ha_s, ha_r, u1_s, u1_r, u2_s, u2_r, u3_s, h1_s, h1_r, hc_s, hc_r, hy_s, hy_r, hf_s, hf_r,
):
    nt, nr, cols, chans, outs, group_size = dims
    pos = 2 * cols
    a = lax.axis_index("tm")
    b = lax.axis_index("rows")
    count = float(nt * nr * pos * group_size)

    nq = chans // 128
    f_copy = pltpu.make_async_copy(feat_hbm, feat, in_sem.at[0])
    c_copy = pltpu.make_async_copy(up_hbm, up_ref, in_sem.at[1])
    g_copy = pltpu.make_async_copy(gain_hbm, gain_ref, in_sem.at[2])
    b_copy = pltpu.make_async_copy(bias_hbm, bias_ref, in_sem.at[3])
    w_copy = pltpu.make_async_copy(weight_hbm, weight, in_sem.at[4])
    f_copy.start()
    c_copy.start()
    g_copy.start()
    b_copy.start()

    barrier = pltpu.get_barrier_semaphore()
    tm_peers = [lax.rem(a + d, nt) for d in range(1, nt)]
    row_peers = [lax.rem(b + d, nr) for d in range(1, nr)]
    line_peers = [lax.rem(a + d, nt) for d in range(2, nt, 2)]
    side = a + 1 - 2 * lax.rem(a, 2)
    twin = b + 1 - 2 * lax.rem(b, 2)
    across = lax.rem(b + 2, nr)
    far = lax.rem(twin + 2, nr)
    for peer in row_peers:
        pl.semaphore_signal(barrier, inc=1, device_id=(a, peer), device_id_type=MESH)
    for peer in tm_peers:
        pl.semaphore_signal(barrier, inc=1, device_id=(peer, b), device_id_type=MESH)

    def to_row(src, dst, ssem, rsem, peer):
        return pltpu.make_async_remote_copy(
            src_ref=src, dst_ref=dst, send_sem=ssem, recv_sem=rsem,
            device_id=(a, peer), device_id_type=MESH,
        )

    def to_tm(src, dst, ssem, rsem, peer):
        return pltpu.make_async_remote_copy(
            src_ref=src, dst_ref=dst, send_sem=ssem, recv_sem=rsem,
            device_id=(peer, b), device_id_type=MESH,
        )

    f_copy.wait()
    w_copy.start()
    for q in range(nq):
        xs = feat[:, q * 128 : q * 128 + 128].astype(F32)
        st_r[b, q : q + 1] = jnp.sum(xs, axis=0, keepdims=True)
        st_r[b, nq + q : nq + q + 1] = jnp.sum(xs * xs, axis=0, keepdims=True)
    pl.semaphore_wait(barrier, nt + nr - 2)
    for peer in row_peers:
        to_row(st_r.at[b], st_r.at[b], st_rs.at[peer], st_rr.at[b], peer).start()

    c_copy.wait()
    for q in range(outs // 128):
        lanes = slice(q * 128, q * 128 + 128)
        even, odd = pack_pair(
            up_ref[0:cols, lanes].astype(F32), up_ref[cols:pos, lanes].astype(F32)
        )
        upack[2 * q] = even
        upack[2 * q + 1] = odd
    def u1_copy(src_row, peer):
        return to_row(
            upack.at[peer], uall.at[src_row, pl.ds(a * cols, cols)],
            u1_s.at[peer], u1_r.at[src_row], peer,
        )

    for peer in row_peers:
        u1_copy(b, peer).start()
    own = pl.ds(pl.multiple_of(a * cols, 32), cols)
    uall[b, own] = upack[b]

    here, ahead_rows = pl.ds(0, pos), pl.ds(pos, pos)
    above, below = lax.rem(b + nr - 1, nr), lax.rem(b + 1, nr)

    def to_above():
        return to_row(up_ref, ext.at[2, here], ha_s.at[0], ha_r.at[0], above)

    def to_below():
        return to_row(up_ref, ext.at[0, here], ha_s.at[1], ha_r.at[1], below)

    def to_earlier():
        return to_tm(
            up_ref, ext.at[1, ahead_rows], ha_s.at[2], ha_r.at[2], lax.rem(a + nt - 1, nt)
        )

    def next_above():
        return to_row(
            ext.at[1, ahead_rows], ext.at[2, ahead_rows], ha_s.at[3], ha_r.at[3], above
        )

    def next_below():
        return to_row(
            ext.at[1, ahead_rows], ext.at[0, ahead_rows], ha_s.at[4], ha_r.at[4], below
        )

    not_top, not_bottom = b > 0, b < nr - 1
    not_first, not_last = a > 0, a < nt - 1

    @pl.when(not_first)
    def _():
        to_earlier().start()

    @pl.when(not_top)
    def _():
        to_above().start()

    @pl.when(not_bottom)
    def _():
        to_below().start()

    ext[1, 0:pos] = up_ref[...]
    zeros_ext = jnp.zeros((2 * pos, outs), BF16)

    @pl.when(b == 0)
    def _():
        ext[0] = zeros_ext

    @pl.when(b == nr - 1)
    def _():
        ext[2] = zeros_ext

    @pl.when(a == nt - 1)
    def _():
        for r in range(3):
            ext[r, pos : 2 * pos] = zeros_ext[0:pos]

    for peer in row_peers:
        to_row(st_r.at[b], st_r.at[peer], st_rs.at[peer], st_rr.at[peer], peer).wait_recv()
    part = st_r[0]
    for r in range(1, nr):
        part = part + st_r[r]
    st_t[a] = part
    for peer in tm_peers:
        to_tm(st_t.at[a], st_t.at[a], st_ts.at[peer], st_tr.at[a], peer).start()

    for peer in row_peers:
        u1_copy(peer, peer).wait_recv()

    def u2_copy(src, peer, ssem):
        place = pl.ds(src * cols, cols)
        return to_tm(
            uall.at[:, place], uall.at[:, place], ssem, u2_r.at[src], peer
        )

    def u3_copy(src):
        place = pl.ds(src * cols, cols)
        return to_tm(
            uall.at[:, place], uall.at[:, place], u3_s.at[src], u2_r.at[src], side
        )

    @pl.when(a + 2 < nt)
    def _():
        u2_copy(a, lax.rem(a + 2, nt), u2_s.at[a]).start()

    @pl.when(a >= 2)
    def _():
        u2_copy(a, lax.rem(a + nt - 2, nt), u2_s.at[side]).start()

    u3_copy(a).start()

    for peer in tm_peers:
        to_tm(st_t.at[a], st_t.at[peer], st_ts.at[peer], st_tr.at[peer], peer).wait_recv()
    total = st_t[0]
    for t in range(1, nt):
        total = total + st_t[t]
    total = group_total(total, group_size) / count
    centre = total[0:nq]
    inverse = lax.rsqrt(total[nq : 2 * nq] - centre * centre + epsilon)
    g_copy.wait()
    b_copy.wait()
    for q in range(nq):
        lanes = slice(q * 128, q * 128 + 128)
        halves = []
        for f in range(2):
            rows = slice(f * cols, f * cols + cols)
            normed = (feat[rows, lanes].astype(F32) - centre[q : q + 1]) * inverse[q : q + 1]
            preact = normed * gain_ref[:, lanes] + bias_ref[:, lanes]
            sig = jax.nn.sigmoid(preact)
            normed_s[rows, lanes] = normed
            dact_s[rows, lanes] = sig * (1.0 + preact * (1.0 - sig))
            halves.append(preact * sig)
        even, odd = pack_pair(*halves)
        hpack[2 * q] = even
        hpack[2 * q + 1] = odd

    def h1_copy(src, peer):
        return to_tm(
            hpack.at[peer], hall.at[b, pl.ds((src + 1) * cols, cols)],
            h1_s.at[peer], h1_r.at[src], peer,
        )

    for peer in tm_peers:
        h1_copy(a, peer).start()
    hall[b, pl.ds(pl.multiple_of((a + 1) * cols, 32), cols)] = hpack[a]

    @pl.when(not_last)
    def _():
        to_earlier().wait_recv()

    @pl.when(not_last & not_top)
    def _():
        next_above().start()

    @pl.when(not_last & not_bottom)
    def _():
        next_below().start()

    @pl.when(not_top)
    def _():
        to_below().wait_recv()

    @pl.when(not_bottom)
    def _():
        to_above().wait_recv()

    w_copy.wait()

    def dot_t(lhs, rhs):
        return lax.dot_general(lhs, rhs, (((1,), (1,)), ((), ())), preferred_element_type=F32)

    def dense_own(c, carry):
        val = dot_t(ext[2, 0:pos], weight[2, 0, c])
        for tap in range(1, 3):
            val = val + dot_t(ext[2 - tap, 0:pos], weight[2, tap, c])
        acc[c] = val
        return carry

    lax.fori_loop(0, 3, dense_own, 0)


    def pass_on(row, src, ssem, rsem, peer):
        place = hall.at[row, pl.ds((src + 1) * cols, cols)]
        return to_row(place, place, ssem.at[src], rsem.at[src], peer)

    pass_on(b, a, hy_s, hy_r, across).start()
    pass_on(b, a, hc_s, hc_r, twin).start()
    for peer in tm_peers:
        h1_copy(peer, peer).wait_recv()
        pass_on(b, peer, hy_s, hy_r, across).start()
        pass_on(b, peer, hc_s, hc_r, twin).start()

    for d in range(1, nt // 2):
        src_low, src_high = a - 2 * d, a + 2 * d

        @pl.when(src_low >= 0)
        def _(src=src_low):
            u2_copy(src, a, u2_s.at[a]).wait_recv()

            @pl.when(a + 2 < nt)
            def _():
                u2_copy(src, lax.rem(a + 2, nt), u2_s.at[src]).start()

            u3_copy(src).start()

        @pl.when(src_high < nt)
        def _(src=src_high):
            u2_copy(src, a, u2_s.at[a]).wait_recv()

            @pl.when(a >= 2)
            def _():
                u2_copy(src, lax.rem(a + nt - 2, nt), u2_s.at[src]).start()

            u3_copy(src).start()

    @pl.when(not_last & not_top)
    def _():
        next_below().wait_recv()

    @pl.when(not_last & not_bottom)
    def _():
        next_above().wait_recv()

    def dense_rest(c, carry):
        val = acc[c]
        for tap in range(3):
            val = val + dot_t(ext[2 - tap, cols : cols + pos], weight[1, tap, c])
            val = val + dot_t(ext[2 - tap, pos : 2 * pos], weight[0, tap, c])
        acc[c] = val
        return carry

    lax.fori_loop(0, 3, dense_rest, 0)

    @pl.when(a == 0)
    def _():
        def dense_first(c, carry):
            val = acc[c, 0:cols]
            for tap in range(3):
                val = val + dot_t(ext[2 - tap, 0:cols], weight[0, tap, c])
                val = val + dot_t(ext[2 - tap, 0:cols], weight[1, tap, c])
                val = val + dot_t(ext[2 - tap, cols:pos], weight[0, tap, c])
            acc[c, 0:cols] = val
            return carry

        lax.fori_loop(0, 3, dense_first, 0)

    for src in [a] + tm_peers:
        pass_on(across, src, hy_s, hy_r, across).wait_recv()
        pass_on(across, src, hf_s, hf_r, twin).start()

    for q in range(chans // 128):
        lanes = slice(q * 128, q * 128 + 128)
        sum_gain = jnp.zeros((1, 128), F32)
        sum_bias = jnp.zeros((1, 128), F32)
        for f in range(2):
            rows = slice(f * cols, f * cols + cols)
            place = lax.broadcasted_iota(jnp.int32, (cols, 128), 0)
            right = jnp.where(
                place == cols - 1, 0.0, pltpu.roll(acc[0, rows, lanes], cols - 1, 0)
            )
            left = jnp.where(place == 0, 0.0, pltpu.roll(acc[2, rows, lanes], 1, 0))
            act = (acc[1, rows, lanes] + right + left) * dact_s[rows, lanes]
            dact_s[rows, lanes] = act
            sum_gain = sum_gain + jnp.sum(act * normed_s[rows, lanes], axis=0, keepdims=True)
            sum_bias = sum_bias + jnp.sum(act, axis=0, keepdims=True)
        sg_r[b, q : q + 1] = sum_gain
        sg_r[b, nq + q : nq + q + 1] = sum_bias
    for peer in row_peers:
        to_row(sg_r.at[b], sg_r.at[b], sg_rs.at[peer], sg_rr.at[b], peer).start()

    for src in [side] + [lax.rem(side + d, nt) for d in range(2, nt, 2)]:
        u3_copy(src).wait_recv()
    half = nt * cols // 2
    for part_index in range(2):
        rows = slice(part_index * half, part_index * half + half)
        place = lax.broadcasted_iota(jnp.int32, (half, 128), 0) % cols

        def turn(i, carry, rows=rows, place=place):
            block = uall[i, rows].astype(F32)
            ahead = jnp.where(place == cols - 1, 0.0, pltpu.roll(block, half - 1, 0))
            behind = jnp.where(place == 0, 0.0, pltpu.roll(block, 1, 0))
            ut[i, 0:128, rows] = ahead.T.astype(BF16)
            ut[i, 128:256, rows] = block.T.astype(BF16)
            ut[i, 256:384, rows] = behind.T.astype(BF16)
            return carry

        lax.fori_loop(0, nr, turn, 0)

    for peer in row_peers:
        to_row(sg_r.at[b], sg_r.at[peer], sg_rs.at[peer], sg_rr.at[peer], peer).wait_recv()
    part = sg_r[0]
    for r in range(1, nr):
        part = part + sg_r[r]
    sg_t[a] = part
    for peer in tm_peers:
        to_tm(sg_t.at[a], sg_t.at[a], sg_ts.at[peer], sg_tr.at[a], peer).start()

    for src in [a] + tm_peers:
        pass_on(twin, src, hc_s, hc_r, twin).wait_recv()
        pass_on(far, src, hf_s, hf_r, twin).wait_recv()
    low = lax.broadcasted_iota(jnp.int32, (cols, 128), 1) < 64
    for r in range(nr):
        block = hall[r, cols : 2 * cols].astype(F32)
        hall[r, 0:cols] = jnp.where(low, block, pltpu.roll(block, 64, 1)).astype(BF16)
    span = nt * cols
    for r in range(nr):
        both = jnp.concatenate([hall[r, 0:span], hall[r, cols : cols + span]], axis=1)
        for tap in range(3):
            i = r - tap + 1
            if 0 <= i < nr:
                prod = jnp.dot(ut[i], both, preferred_element_type=F32)
                first = r == max(0, tap - 1)
                gacc[tap] = prod if first else gacc[tap] + prod
    for tap in range(3):
        for c in range(3):
            base = c * 128
            even = gacc[tap, base : base + 64]
            odd = gacc[tap, base + 64 : base + 128]
            turned = (even + pltpu.roll(odd, 192, 1)).T
            for t in range(3):
                gw_ref[t * 9 + tap * 3 + c] = turned[t * 64 : t * 64 + 64]

    for peer in tm_peers:
        to_tm(sg_t.at[a], sg_t.at[peer], sg_ts.at[peer], sg_tr.at[peer], peer).wait_recv()
    total = sg_t[0]
    for t in range(1, nt):
        total = total + sg_t[t]
    for q in range(nq):
        lanes = slice(q * 128, q * 128 + 128)
        gain = gain_ref[:, lanes]
        gg_ref[:, lanes] = total[q : q + 1]
        gb_ref[:, lanes] = total[nq + q : nq + q + 1]
        second_term = group_total(total[q : q + 1] * gain, group_size) / count
        first_term = group_total(total[nq + q : nq + q + 1] * gain, group_size) / count
        gf_ref[:, lanes] = (
            inverse[q : q + 1]
            * (dact_s[:, lanes] * gain - first_term - normed_s[:, lanes] * second_term)
        ).astype(BF16)

    for peer in row_peers:
        to_row(st_r.at[b], st_r.at[b], st_rs.at[peer], st_rr.at[b], peer).wait_send()
        to_row(sg_r.at[b], sg_r.at[b], sg_rs.at[peer], sg_rr.at[b], peer).wait_send()
        u1_copy(b, peer).wait_send()
    for peer in tm_peers:
        to_tm(st_t.at[a], st_t.at[a], st_ts.at[peer], st_tr.at[a], peer).wait_send()
        to_tm(sg_t.at[a], sg_t.at[a], sg_ts.at[peer], sg_tr.at[a], peer).wait_send()
        h1_copy(a, peer).wait_send()
    u3_copy(a).wait_send()
    for peer in line_peers:
        u3_copy(peer).wait_send()

    @pl.when(a + 2 < nt)
    def _():
        u2_copy(a, lax.rem(a + 2, nt), u2_s.at[a]).wait_send()

    @pl.when(a >= 2)
    def _():
        u2_copy(a, lax.rem(a + nt - 2, nt), u2_s.at[side]).wait_send()

    for d in range(1, nt // 2):
        @pl.when((a - 2 * d >= 0) & (a + 2 < nt))
        def _(src=a - 2 * d):
            u2_copy(src, lax.rem(a + 2, nt), u2_s.at[src]).wait_send()

        @pl.when((a + 2 * d < nt) & (a >= 2))
        def _(src=a + 2 * d):
            u2_copy(src, lax.rem(a + nt - 2, nt), u2_s.at[src]).wait_send()
    for src in [a] + tm_peers:
        pass_on(b, src, hy_s, hy_r, across).wait_send()
        pass_on(b, src, hc_s, hc_r, twin).wait_send()
        pass_on(across, src, hf_s, hf_r, twin).wait_send()

    @pl.when(not_top)
    def _():
        to_above().wait_send()

    @pl.when(not_bottom)
    def _():
        to_below().wait_send()

    @pl.when(not_first)
    def _():
        to_earlier().wait_send()

    @pl.when(not_last & not_top)
    def _():
        next_above().wait_send()

    @pl.when(not_last & not_bottom)
    def _():
        next_below().wait_send()


def fused(features, norm_gain, norm_bias, weight, upstream):
    frames_dev, rows_dev, cols, chans = features.shape
    outs = upstream.shape[3]
    nt, nr = lax.axis_size("tm"), lax.axis_size("rows")
    pos = frames_dev * rows_dev * cols
    dims = (nt, nr, cols, chans, outs, chans // GROUPS)
    vmem = pl.BlockSpec(memory_space=pltpu.VMEM)
    dma = pltpu.SemaphoreType.DMA
    span = nt * cols
    gf, gw, gg, gb = pl.pallas_call(
        functools.partial(kernel, dims),
        out_shape=(
            jax.ShapeDtypeStruct((pos, chans), BF16),
            jax.ShapeDtypeStruct((27, 64, 64), F32),
            jax.ShapeDtypeStruct((1, chans), F32),
            jax.ShapeDtypeStruct((1, chans), F32),
        ),
        in_specs=[pl.BlockSpec(memory_space=pltpu.HBM)] * 5,
        out_specs=(vmem, vmem, vmem, vmem),
        scratch_shapes=[
            pltpu.VMEM((pos, chans), BF16),
            pltpu.VMEM((1, chans), F32),
            pltpu.VMEM((1, chans), F32),
            pltpu.VMEM((pos, outs), BF16),
            pltpu.VMEM((3, 3, 3, chans, outs), BF16),
            pltpu.VMEM((3, 2 * pos, outs), BF16),
            pltpu.VMEM((3, pos, chans), F32),
            pltpu.VMEM((pos, chans), F32),
            pltpu.VMEM((pos, chans), F32),
            pltpu.VMEM((nt, cols, 128), BF16),
            pltpu.VMEM((nr, span + cols, 128), BF16),
            pltpu.VMEM((nr, cols, 128), BF16),
            pltpu.VMEM((nr, span, 128), BF16),
            pltpu.VMEM((nr, 384, span), BF16),
            pltpu.VMEM((3, 384, 256), F32),
            pltpu.VMEM((nr, 8, 128), F32),
            pltpu.VMEM((nt, 8, 128), F32),
            pltpu.VMEM((nr, 8, 128), F32),
            pltpu.VMEM((nt, 8, 128), F32),
            dma((5,)),
            dma((nr,)), dma((nr,)), dma((nt,)), dma((nt,)),
            dma((nr,)), dma((nr,)), dma((nt,)), dma((nt,)),
            dma((5,)), dma((5,)),
            dma((nr,)), dma((nr,)), dma((nt,)), dma((nt,)), dma((nt,)),
            dma((nt,)), dma((nt,)), dma((nt,)), dma((nt,)),
            dma((nt,)), dma((nt,)), dma((nt,)), dma((nt,)),
        ],
        compiler_params=pltpu.CompilerParams(
            collective_id=0, has_side_effects=True, vmem_limit_bytes=48 * 1024 * 1024
        ),
    )(
        features.reshape(pos, chans),
        norm_gain.reshape(1, chans),
        norm_bias.reshape(1, chans),
        weight,
        upstream.reshape(pos, outs),
    )
    return (
        gf.reshape(features.shape),
        gw.reshape(3, 3, 3, 64, 64),
        gg.reshape(chans),
        gb.reshape(chans),
    )


def body(features, norm_gain, norm_bias, weight, upstream):
    frames_dev, rows_dev, cols, chans = features.shape
    outs = upstream.shape[3]
    nt, nr = lax.axis_size("tm"), lax.axis_size("rows")
    fits = (
        CLIPS == 1
        and (frames_dev, rows_dev) == (2, 1)
        and (nt, nr) == (8, 4)
        and (chans, outs) == (64 * nt, 64 * nr)
        and cols % 32 == 0
        and (nt * cols) % 256 == 0
    )
    run = fused if fits else on_device
    return run(features, norm_gain, norm_bias, weight, upstream)


def solution(mesh):
    in_specs = (P("tm", "rows", None, None), P(), P(), P(), P("tm", "rows", None, None))
    out_specs = (P("tm", "rows", None, None), P(None, None, None, "tm", "rows"), P(), P())
    return jax.shard_map(
        body, mesh=mesh, in_specs=in_specs, out_specs=out_specs, check_vma=False
    )
```
